32 devices in a mesh: rep: 8 (over z, x), exp: 4 (over y, core).
Axes of the slice: x: 2, y: 2, z: 4, core: 2. Of those that a mesh axis runs over, the one named last changes fastest.
Arguments:
- tokens: bfloat16 [4096, 2048], P(('rep', 'exp')), may hold values from -6 to 6
- expert_ids: int32 [4096, 1], P(('rep', 'exp')), may hold values from 0 to 3; in each aligned block of 128 rows (0 to 127, 128 to 255, ...) at most 32 rows name the same one
- gate_prob: float32 [4096], P(('rep', 'exp')), may hold values from 0.05 to 1
- cotangent: bfloat16 [4096, 2048], P(('rep', 'exp')), may hold values from -6 to 6
- w_gate: bfloat16 [8, 2048, 4096], P('rep', None, 'exp'), may hold values from -0.125 to 0.125
- w_up: bfloat16 [8, 2048, 4096], P('rep', None, 'exp'), may hold values from -0.125 to 0.125
- w_down: bfloat16 [8, 4096, 2048], P('rep', 'exp'), may hold values from -0.1875 to 0.1875
- touched: int32 [8, 256], P('rep', 'exp'), may hold values 0 or 1
Outputs:
- mixed: bfloat16 [4096, 2048], P(('rep', 'exp'))
- averaged: bfloat16 [4096, 6144], P('exp', 'rep')
The draws below stay inside these ranges and needn't reach their ends.
Inputs may be any that keep to these rules, and one draw needn't show every extreme that they name: `expert_ids`: the rows of one device name each of the 4 window experts exactly 32 times.
All inputs are finite; a program needn't handle non-finite values. No bound on the sum of `touched` on one device may be relied on, other than what follows from the above.
Results may differ from the reference program's by a relative error of at most 0.018.
Values may be sent and summed in bfloat16 or wider, within the bound.
A program may use at most 128 MiB of HBM per device.

```python
import math
import jax
import jax.numpy as jnp
import numpy as np
from jax import lax

D = 2048
FF = 1024
EW = 4
TILE = 16
ROWS_DEV = 128
CAP = 32
SHARDS = 1
HID = 1024
NTILE = 256
REPS = 8
TOKENS = 4096
N_EXP = 4


def plant(drawn, rng, smallest, largest):
    spot = [jax.random.randint(jax.random.fold_in(rng, axis), (), 0, length) for axis, length in enumerate(drawn.shape)]
    longest = drawn.shape.index(max(drawn.shape))
    neighbour = spot[:longest] + [(spot[longest] + 1) % drawn.shape[longest]] + spot[longest + 1:]
    return drawn.at[tuple(spot)].set(smallest).at[tuple(neighbour)].set(largest)


def block_levels(own_key, shape, cuts, low, top_value):
    def one(dim, blocks):
        draws = jax.random.uniform(jax.random.fold_in(jax.random.fold_in(own_key, 6), dim), (blocks,), jnp.float32, low / len(cuts), top_value / len(cuts))
        return jnp.repeat(jnp.exp(draws), shape[dim] // blocks).reshape((-1,) + (1,) * (len(shape) - dim - 1))

    gain = one(*cuts[0])
    for cut in cuts[1:]:
        gain = gain * one(*cut)
    return gain


def routed_block(stream_key, own, number, rows, count, top, limit, lean):
    sequence = jax.random.permutation(stream_key, count)
    heavy_load, usual = portions_of(count, rows * top, limit, lean, True), portions_of(count, rows * top, limit, lean, False)
    places = jnp.arange(count)

    def named(sizes, offset_by):
        used = int((sizes > 0).sum())
        fixed = max(1, used // 4)
        moved = fixed + (places - fixed + offset_by * (used - fixed)) % max(1, count - fixed)
        return jnp.zeros((count,), jnp.int32).at[sequence[jnp.where(places < fixed, places, moved)]].set(jnp.asarray(sizes, jnp.int32))

    sizes = jnp.where(number % 4 == 0, named(heavy_load, number // 4), named(usual, number - number // 4 - 1))
    mixed = jax.random.permutation(jax.random.fold_in(own, 3), count)
    donor, sink = mixed[0:count // 2 * 2:2], mixed[1:count // 2 * 2:2]
    room = jnp.minimum(sizes[donor] - 1, limit - sizes[sink]) // 2
    room = jnp.where((donor == sequence[0]) | (sink == sequence[0]) | (sizes[sink] == 0), 0, jnp.maximum(room, 0))
    moved = jax.random.randint(jax.random.fold_in(own, 4), (count // 2,), 0, 1 << 20) % (room + 1)
    sizes = sizes.at[donor].add(-moved).at[sink].add(moved)
    labels = jnp.searchsorted(jnp.cumsum(sizes), jnp.arange(rows * top), side="right").astype(jnp.int32)
    table = labels.reshape(top, rows).T
    table = table[jax.random.permutation(jax.random.fold_in(own, 1), rows)]
    offset_by = jax.random.randint(jax.random.fold_in(own, 2), (rows, 1), 0, top)
    return jnp.take_along_axis(table, (jnp.arange(top)[None, :] + offset_by) % top, axis=1)


def portions_of(count, total, most, lean, full):
    portions = [(1 << 20) // math.isqrt(standing ** lean) + 1 for standing in range(1, count + 1)]
    largest = most if full else min(most, max(-(-total // count), total * portions[0] // sum(portions)))
    least = 1 if total - largest >= count - 1 else 0
    given, surplus = [largest] + [least] * (count - 1), total - largest - least * (count - 1)
    while surplus > 0:
        candidates = [i for i in range(1, count) if given[i] < largest] or [i for i in range(1, count) if given[i] < most]
        pool, remaining = sum([portions[i] for i in candidates]), surplus
        for i in candidates:
            more = min(most - given[i], max(1, remaining * portions[i] // pool), surplus)
            given[i] = given[i] + more
            surplus = surplus - more
    return np.array(given)


def bell_draw(stream_key, shape, scale, most, cuts=(), held_as=jnp.bfloat16):
    values = jax.random.normal(stream_key, shape, jnp.float32) * scale
    if len(cuts) > 0:
        values = block_levels(stream_key, shape, cuts, -0.22, 0.18) * values
    return jnp.clip(values, min=-most, max=most).astype(held_as)


def setup_inputs(seed: int = 0) -> dict:
    streams_of = jax.random.split(jax.random.key(seed), 9)
    tokens = bell_draw(streams_of[0], (TOKENS, D), 1.0, 6.0, ((0, 32),))
    expert_ids_keys = jax.random.split(jax.random.fold_in(streams_of[1], 1), TOKENS // ROWS_DEV)
    expert_ids_turns = jax.random.permutation(jax.random.fold_in(streams_of[1], 3), TOKENS // ROWS_DEV)
    expert_ids = jax.vmap(lambda own, number: routed_block(jax.random.fold_in(streams_of[1], 2), own, number, ROWS_DEV, EW, 1, CAP, 0))(expert_ids_keys, expert_ids_turns).reshape((TOKENS, 1))
    gate_prob = jnp.clip(jnp.exp(math.log(1.0) - 2.9957323 * jax.random.uniform(streams_of[2], (TOKENS,), jnp.float32) ** block_levels(streams_of[2], (TOKENS,), ((0, 32),), -0.2, 0.2)), 0.05, 1.0)
    cotangent = bell_draw(streams_of[3], (TOKENS, D), 1.0, 6.0, ((0, 32),))
    w_gate = bell_draw(streams_of[4], (REPS, D, EW * FF), D ** -0.5, 0.125, ((0, 8), (2, 4)))
    w_up = bell_draw(streams_of[5], (REPS, D, EW * FF), D ** -0.5, 0.125, ((0, 8), (2, 4)))
    w_down = bell_draw(streams_of[6], (REPS, EW * FF, D), FF ** -0.5, 0.1875, ((0, 8), (1, 4)))
    touched = plant((jax.random.randint(streams_of[7], (REPS, NTILE), 0, 2) < 1).astype(jnp.int32), jax.random.fold_in(streams_of[7], 1), 0, 1)
    return {"tokens": tokens, "expert_ids": expert_ids, "gate_prob": gate_prob, "cotangent": cotangent, "w_gate": w_gate, "w_up": w_up, "w_down": w_down, "touched": touched}


def swish_slope(h):
    s = jax.nn.sigmoid(h)
    return s * (1.0 + h * (1.0 - s))


def one_replica(xrows, ids, gate, cot, wg, wu, wd, mask):
    dy = (gate[:, None] * cot.astype(jnp.float32)).astype(jnp.bfloat16)
    mixed = jnp.zeros(xrows.shape, jnp.float32)
    blocks = []
    for e in range(EW):
        rows_e = ids[:, 0] == e
        wg_e = wg[:, e * FF:(e + 1) * FF]
        wu_e = wu[:, e * FF:(e + 1) * FF]
        wd_e = wd[e * FF:(e + 1) * FF, :]
        h = jnp.dot(xrows, wg_e, preferred_element_type=jnp.float32)
        u = jnp.dot(xrows, wu_e, preferred_element_type=jnp.float32)
        act = (h * jax.nn.sigmoid(h) * u).astype(jnp.bfloat16)
        total = jnp.zeros(xrows.shape, jnp.float32)
        for s in range(SHARDS):
            part = jnp.dot(act[:, s * HID:(s + 1) * HID], wd_e[s * HID:(s + 1) * HID, :],
                           preferred_element_type=jnp.float32).astype(jnp.bfloat16)
            part = lax.optimization_barrier(part)
            total = total + part.astype(jnp.float32)
        mixed = jnp.where(rows_e[:, None], gate[:, None] * total, mixed)
        dy_e = jnp.where(rows_e[:, None], dy, jnp.zeros_like(dy))
        grad_a = jnp.dot(dy_e, wd_e.T, preferred_element_type=jnp.float32)
        d_down = jnp.dot(act.T, dy_e, preferred_element_type=jnp.float32)
        d_h = (grad_a * u * swish_slope(h)).astype(jnp.bfloat16)
        d_u = (grad_a * h * jax.nn.sigmoid(h)).astype(jnp.bfloat16)
        d_gate = jnp.dot(d_h.T, xrows, preferred_element_type=jnp.float32)
        d_upper = jnp.dot(d_u.T, xrows, preferred_element_type=jnp.float32)
        blocks.append(jnp.concatenate([d_gate, d_upper, d_down], axis=1))
    delta = jnp.concatenate(blocks, axis=0)
    scale = jnp.repeat(mask.astype(jnp.float32), TILE)
    rounded = lax.optimization_barrier((delta * scale[:, None]).astype(jnp.bfloat16))
    return mixed.astype(jnp.bfloat16), rounded


def reference(tokens, expert_ids, gate_prob, cotangent, w_gate, w_up, w_down, touched):
    per = N_EXP * ROWS_DEV
    xs = tokens.reshape(REPS, per, D)
    ids = expert_ids.reshape(REPS, per, 1)
    gates = gate_prob.reshape(REPS, per)
    cots = cotangent.reshape(REPS, per, D)

    def step(acc, items):
        xrows, idr, gate, cot, wg, wu, wd, mask = items
        mixed, delta = one_replica(xrows, idr, gate, cot, wg, wu, wd, mask)
        return acc + delta.astype(jnp.float32), mixed

    init = jnp.zeros((EW * FF, 3 * D), jnp.float32)
    acc, mixed = lax.scan(step, init, (xs, ids, gates, cots, w_gate, w_up, w_down, touched))
    averaged = (acc / REPS).astype(jnp.bfloat16)
    return mixed.reshape(TOKENS, D), averaged
```

```python
import functools
import math

import jax
import jax.numpy as jnp
from jax import lax
from jax.experimental import pallas as pl
from jax.experimental.pallas import tpu as pltpu
from jax.sharding import PartitionSpec as P

EW = 4
TILE = 16
PIECES = 8
AHEAD = 2
B_LAG = 2
F32 = jnp.float32
BF16 = jnp.bfloat16


def swish_slope(h):
    s = jax.nn.sigmoid(h)
    return s * (1.0 + h * (1.0 - s))


def reduce_kernel(
    n, l_ref, r_ref, out_ref, xsend, xrecv, up, down, own_b, up_b, down_b, xs_b, xr_b,
    xs_sem, xr_sem, us_sem, ur_sem, ds_sem, dr_sem,
    bus_sem, bur_sem, bds_sem, bdr_sem, bx_sem,
):
    na = PIECES - 1
    n_rep = 2 * n
    tpc = xsend.shape[2]
    tw = xsend.shape[4]
    pr = xsend.shape[3]
    tpw = r_ref.shape[0] // 2
    rep = lax.axis_index("rep")
    z = rep // 2
    x = rep % 2
    peer = {"rep": rep + 1 - 2 * x}
    above = {"rep": jnp.minimum(rep + 2, n_rep - 1)}
    below = {"rep": jnp.maximum(rep - 2, 0)}
    last = n - 1
    b_lag = B_LAG if B_LAG * last < na + last else 1

    def part(p, r, j):
        t = r * tpc + j
        mat = t // tpw
        src = t % tpw + jnp.where(mat == 2, tpw, 0)
        return jnp.dot(l_ref[mat, p], r_ref[src], preferred_element_type=F32)

    def remote(src, dst, send, recv, dev):
        return pltpu.make_async_remote_copy(
            src_ref=src, dst_ref=dst, send_sem=send, recv_sem=recv,
            device_id=dev, device_id_type=pl.DeviceIdType.MESH,
        )

    def x_copy(p):
        return remote(xsend.at[p], xrecv.at[p], xs_sem.at[p], xr_sem.at[p], peer)

    def up_copy(src, p, d):
        return remote(src.at[p, d], up.at[p, d], us_sem.at[p, d], ur_sem.at[p, d], above)

    def down_copy(src, p, d):
        return remote(src.at[p, d], down.at[p, d], ds_sem.at[p, d], dr_sem.at[p, d], below)

    def upb_copy(src, d):
        return remote(src.at[d], up_b.at[d], bus_sem.at[d], bur_sem.at[d], above)

    def downb_copy(src, d):
        return remote(src.at[d], down_b.at[d], bds_sem.at[d], bdr_sem.at[d], below)

    def xb_copy():
        return remote(xs_b, xr_b, bx_sem.at[0], bx_sem.at[1], peer)

    barrier = pltpu.get_barrier_semaphore()
    mesh_id = pl.DeviceIdType.MESH
    pl.semaphore_signal(barrier, inc=1, device_id=peer, device_id_type=mesh_id)

    @pl.when(z < last)
    def _():
        pl.semaphore_signal(barrier, inc=1, device_id=above, device_id_type=mesh_id)

    @pl.when(z > 0)
    def _():
        pl.semaphore_signal(barrier, inc=1, device_id=below, device_id_type=mesh_id)

    pl.semaphore_wait(barrier, 1 + jnp.where(z < last, 1, 0) + jnp.where(z > 0, 1, 0))

    def send_x(p):
        def one(d, c):
            for j in range(tpc):
                xsend[p, d, j] = part(p, 2 * d + 1 - x, j).astype(BF16)
            return c

        lax.fori_loop(0, n, one, 0)
        x_copy(p).start()

    send_x(0)

    def build_b(r, c):
        for j in range(tpc):
            own_b[r // 2, r % 2, j] = part(na, r, j).astype(BF16)
        return c

    lax.fori_loop(0, n_rep, build_b, 0)

    @pl.when(z == 0)
    def _():
        for d in range(last, 0, -1):
            upb_copy(own_b, d).start()

    @pl.when(z == last)
    def _():
        for d in range(last):
            downb_copy(own_b, d).start()

    for p in range(1, AHEAD):
        send_x(p)

    def add_into(dst, src):
        for j in range(tpc):
            dst[j] = (dst[j].astype(F32) + src[j].astype(F32)).astype(BF16)

    def step(i, carry):
        @pl.when(i + AHEAD < na)
        def _():
            send_x(i + AHEAD)

        @pl.when(i < na)
        def _():
            x_copy(i).wait_recv()

            def one(d, c):
                for j in range(tpc):
                    xrecv[i, d, j] = (part(i, 2 * d + x, j) + xrecv[i, d, j].astype(F32)).astype(BF16)
                return c

            lax.fori_loop(0, n, one, 0)

            @pl.when(z == 0)
            def _():
                for d in range(last, 0, -1):
                    up_copy(xrecv, i, d).start()

            @pl.when(z == last)
            def _():
                for d in range(last):
                    down_copy(xrecv, i, d).start()

        q = i - z

        @pl.when((z > 0) & (z < last) & (q >= 0) & (q < na))
        def _():
            for d in range(last, 1, -1):
                @pl.when(d > z)
                def _():
                    up_copy(up, q, d).wait_recv()
                    add_into(up.at[q, d], xrecv.at[q, d])
                    up_copy(up, q, d).start()

        w = i - (last - z)

        @pl.when((z > 0) & (z < last) & (w >= 0) & (w < na))
        def _():
            for d in range(last - 1):
                @pl.when(d < z)
                def _():
                    down_copy(down, w, d).wait_recv()
                    add_into(down.at[w, d], xrecv.at[w, d])
                    down_copy(down, w, d).start()

        f = i - last

        @pl.when((f >= 0) & (f < na))
        def _():
            @pl.when(z > 0)
            def _():
                up_copy(up, f, z).wait_recv()

            @pl.when(z < last)
            def _():
                down_copy(down, f, z).wait_recv()

            for j in range(tpc):
                total = xrecv[f, z, j].astype(F32)
                total += jnp.where(z > 0, up[f, z, j].astype(F32), 0.0)
                total += jnp.where(z < last, down[f, z, j].astype(F32), 0.0)
                out_ref[f, :, j * tw:(j + 1) * tw] = (total / n_rep).astype(BF16)

        @pl.when((z > 0) & (z < last) & (i == b_lag * z))
        def _():
            for d in range(last, 1, -1):
                @pl.when(d > z)
                def _():
                    upb_copy(up_b, d).wait_recv()
                    for k in range(2):
                        add_into(up_b.at[d, k], own_b.at[d, k])
                    upb_copy(up_b, d).start()

        @pl.when((z > 0) & (z < last) & (i == b_lag * (last - z)))
        def _():
            for d in range(last - 1):
                @pl.when(d < z)
                def _():
                    downb_copy(down_b, d).wait_recv()
                    for k in range(2):
                        add_into(down_b.at[d, k], own_b.at[d, k])
                    downb_copy(down_b, d).start()

        @pl.when(i == b_lag * last)
        def _():
            @pl.when(z > 0)
            def _():
                upb_copy(up_b, z).wait_recv()

            @pl.when(z < last)
            def _():
                downb_copy(down_b, z).wait_recv()

            for k in range(2):
                for j in range(tpc):
                    total = own_b[z, k, j].astype(F32)
                    total += jnp.where(z > 0, up_b[z, k, j].astype(F32), 0.0)
                    total += jnp.where(z < last, down_b[z, k, j].astype(F32), 0.0)
                    own_b[z, k, j] = total.astype(BF16)
            for j in range(tpc):
                xs_b[j] = own_b[z, 1 - x, j]
            xb_copy().start()

        return carry

    lax.fori_loop(0, na + last, step, 0)

    xb_copy().wait_recv()
    for j in range(tpc):
        total = own_b[z, x, j].astype(F32) + xr_b[j].astype(F32)
        out_ref[na, :, j * tw:(j + 1) * tw] = (total / n_rep).astype(BF16)
    xb_copy().wait_send()

    def drain(i, carry):
        x_copy(i).wait_send()

        @pl.when(z < last)
        def _():
            for d in range(1, n):
                @pl.when(d > z)
                def _():
                    up_copy(up, i, d).wait_send()

        @pl.when(z > 0)
        def _():
            for d in range(last):
                @pl.when(d < z)
                def _():
                    down_copy(down, i, d).wait_send()

        return carry

    lax.fori_loop(0, na, drain, 0)

    @pl.when(z < last)
    def _():
        for d in range(1, n):
            @pl.when(d > z)
            def _():
                upb_copy(up_b, d).wait_send()

    @pl.when(z > 0)
    def _():
        for d in range(last):
            @pl.when(d < z)
            def _():
                downb_copy(down_b, d).wait_send()


def reduce_deltas(left, right, n_rep, columns):
    n = n_rep // 2
    pr, depth = left.shape[2:]
    tw = right.shape[2]
    tpc = columns // tw
    na = PIECES - 1
    chunk = (tpc, pr, tw)
    dma = pltpu.SemaphoreType.DMA
    vmem = pl.BlockSpec(memory_space=pltpu.VMEM)
    out = pl.pallas_call(
        functools.partial(reduce_kernel, n),
        out_shape=jax.ShapeDtypeStruct((PIECES, pr, columns), BF16),
        in_specs=[vmem] * 2,
        out_specs=vmem,
        scratch_shapes=[
            pltpu.VMEM((na, n) + chunk, BF16),
            pltpu.VMEM((na, n) + chunk, BF16),
            pltpu.VMEM((na, n) + chunk, BF16),
            pltpu.VMEM((na, n) + chunk, BF16),
            pltpu.VMEM((n, 2) + chunk, BF16),
            pltpu.VMEM((n, 2) + chunk, BF16),
            pltpu.VMEM((n, 2) + chunk, BF16),
            pltpu.VMEM(chunk, BF16),
            pltpu.VMEM(chunk, BF16),
            dma((na,)),
            dma((na,)),
            dma((na, n)),
            dma((na, n)),
            dma((na, n)),
            dma((na, n)),
            dma((n,)),
            dma((n,)),
            dma((n,)),
            dma((n,)),
            dma((2,)),
        ],
        compiler_params=pltpu.CompilerParams(
            collective_id=0, has_side_effects=True, vmem_limit_bytes=56 * 2**20
        ),
        cost_estimate=pl.CostEstimate(
            flops=2 * 3 * PIECES * pr * depth * columns * n_rep // 3,
            bytes_accessed=8 * 2**20, transcendentals=0,
        ),
    )(left, right)
    return out.reshape(PIECES * pr, columns)


def body(tokens, expert_ids, gate_prob, cotangent, w_gate, w_up, w_down, touched):
    rows = tokens.shape[0]
    width = tokens.shape[1]
    n_exp = lax.axis_size("exp")
    n_rep = lax.axis_size("rep")
    shards = n_exp // EW
    cap = rows // EW
    onehot = (expert_ids == jnp.arange(EW)[None, :]).astype(jnp.float32)
    lower = (
        lax.broadcasted_iota(jnp.int32, (rows, rows), 0)
        > lax.broadcasted_iota(jnp.int32, (rows, rows), 1)
    ).astype(jnp.float32)
    earlier = jnp.dot(lower, onehot, precision=lax.Precision.HIGHEST)
    slot_of = jnp.sum(onehot * earlier, axis=1).astype(jnp.int32)
    target = expert_ids[:, 0] * cap + slot_of
    placer = (target[None, :] == jnp.arange(EW * cap)[:, None]).astype(jnp.bfloat16)
    dy = (gate_prob[:, None] * cotangent.astype(jnp.float32)).astype(jnp.bfloat16)
    both = jnp.dot(
        placer, jnp.concatenate([tokens, dy], axis=1), preferred_element_type=jnp.float32
    ).astype(jnp.bfloat16).reshape(EW, cap, 2 * width)
    recv = lax.all_to_all(
        jnp.repeat(both, shards, axis=0), "exp", split_axis=0, concat_axis=0, tiled=True
    ).reshape(n_exp * cap, 2 * width)
    x_rows = recv[:, :width]
    d_rows = recv[:, width:]
    wg = w_gate[0]
    wu = w_up[0]
    wd = w_down[0]
    h = jnp.dot(x_rows, wg, preferred_element_type=jnp.float32)
    u = jnp.dot(x_rows, wu, preferred_element_type=jnp.float32)
    act = (h * jax.nn.sigmoid(h) * u).astype(jnp.bfloat16)
    partial_out = jnp.dot(act, wd, preferred_element_type=jnp.float32).astype(jnp.bfloat16)
    returned = lax.all_to_all(
        partial_out.reshape(n_exp, cap, width), "exp", split_axis=0, concat_axis=0, tiled=True
    )
    summed = returned.astype(jnp.float32).reshape(EW, shards, cap, width).sum(axis=1)
    row_out = jnp.take(summed.reshape(EW * cap, width), target, axis=0)
    mixed = (gate_prob[:, None] * row_out).astype(jnp.bfloat16)
    grad_a = lax.dot_general(
        d_rows, wd, (((1,), (1,)), ((), ())), preferred_element_type=jnp.float32
    )
    d_h = (grad_a * u * swish_slope(h)).astype(jnp.bfloat16)
    d_u = (grad_a * h * jax.nn.sigmoid(h)).astype(jnp.bfloat16)
    hidden = d_h.shape[1]
    columns = 3 * width // n_rep
    tw = math.gcd(columns, width)
    mask = jnp.repeat(touched[0], TILE).astype(jnp.bfloat16)
    left = (jnp.stack([d_h, d_u, act]) * mask[None, None, :]).transpose(0, 2, 1)
    left = left.reshape(3, PIECES, hidden // PIECES, left.shape[2])
    right = recv.reshape(recv.shape[0], 2 * width // tw, tw).transpose(1, 0, 2)
    averaged = reduce_deltas(left, right, n_rep, columns)
    return (mixed, averaged)


def solution(mesh):
    return jax.shard_map(
        body,
        mesh=mesh,
        in_specs=(
            P(("rep", "exp"), None),
            P(("rep", "exp"), None),
            P(("rep", "exp")),
            P(("rep", "exp"), None),
            P("rep", None, "exp"),
            P("rep", None, "exp"),
            P("rep", "exp", None),
            P("rep", "exp"),
        ),
        out_specs=(P(("rep", "exp"), None), P("exp", "rep")),
        check_vma=False,
    )
```

```python
import functools
import math

import jax
import jax.numpy as jnp
from jax import lax
from jax.experimental import pallas as pl
from jax.experimental.pallas import tpu as pltpu
from jax.sharding import PartitionSpec as P

EW = 4
TILE = 16
PIECES = 16
N_B = 3
AHEAD = 3
LAG = 2
B_LAG = 2
B_EVERY = 4
F32 = jnp.float32
BF16 = jnp.bfloat16


def swish_slope(h):
    s = jax.nn.sigmoid(h)
    return s * (1.0 + h * (1.0 - s))


def reduce_kernel(
    n, l_ref, r_ref, out_ref, xsend, xrecv, up, down, own_b, up_b, down_b, xs_b, xr_b,
    xs_sem, xr_sem, us_sem, ur_sem, ds_sem, dr_sem,
    bus_sem, bur_sem, bds_sem, bdr_sem, bxs_sem, bxr_sem,
):
    na = PIECES - N_B
    n_rep = 2 * n
    tpc = xsend.shape[2]
    tw = xsend.shape[4]
    pr = xsend.shape[3]
    tpw = r_ref.shape[0] // 2
    rep = lax.axis_index("rep")
    z = rep // 2
    x = rep % 2
    peer = {"rep": rep + 1 - 2 * x}
    above = {"rep": jnp.minimum(rep + 2, n_rep - 1)}
    below = {"rep": jnp.maximum(rep - 2, 0)}
    last = n - 1
    def part(p, r, j):
        t = r * tpc + j
        mat = t // tpw
        src = t % tpw + jnp.where(mat == 2, tpw, 0)
        return jnp.dot(l_ref[mat, p], r_ref[src], preferred_element_type=F32)

    def remote(src, dst, send, recv, dev):
        return pltpu.make_async_remote_copy(
            src_ref=src, dst_ref=dst, send_sem=send, recv_sem=recv,
            device_id=dev, device_id_type=pl.DeviceIdType.MESH,
        )

    def x_copy(p):
        return remote(xsend.at[p], xrecv.at[p], xs_sem.at[p], xr_sem.at[p], peer)

    def up_copy(src, p, d):
        return remote(src.at[p, d], up.at[p, d], us_sem.at[p, d], ur_sem.at[p, d], above)

    def down_copy(src, p, d):
        return remote(src.at[p, d], down.at[p, d], ds_sem.at[p, d], dr_sem.at[p, d], below)

    def upb_copy(src, k, d):
        return remote(src.at[k, d], up_b.at[k, d], bus_sem.at[k, d], bur_sem.at[k, d], above)

    def downb_copy(src, k, d):
        return remote(src.at[k, d], down_b.at[k, d], bds_sem.at[k, d], bdr_sem.at[k, d], below)

    def xb_copy(k):
        return remote(xs_b.at[k], xr_b.at[k], bxs_sem.at[k], bxr_sem.at[k], peer)

    barrier = pltpu.get_barrier_semaphore()
    mesh_id = pl.DeviceIdType.MESH
    pl.semaphore_signal(barrier, inc=1, device_id=peer, device_id_type=mesh_id)

    @pl.when(z < last)
    def _():
        pl.semaphore_signal(barrier, inc=1, device_id=above, device_id_type=mesh_id)

    @pl.when(z > 0)
    def _():
        pl.semaphore_signal(barrier, inc=1, device_id=below, device_id_type=mesh_id)

    pl.semaphore_wait(barrier, 1 + jnp.where(z < last, 1, 0) + jnp.where(z > 0, 1, 0))

    def send_x(p):
        def one(d, c):
            for j in range(tpc):
                xsend[p, d, j] = part(p, 2 * d + 1 - x, j).astype(BF16)
            return c

        lax.fori_loop(0, n, one, 0)
        x_copy(p).start()

    for p in range(AHEAD):
        send_x(p)

    def send_b(k):
        def build_b(r, c):
            for j in range(tpc):
                own_b[k, r // 2, r % 2, j] = part(na + k, r, j).astype(BF16)
            return c

        lax.fori_loop(0, n_rep, build_b, 0)

        @pl.when(z == 0)
        def _():
            for d in range(last, 0, -1):
                upb_copy(own_b, k, d).start()

        @pl.when(z == last)
        def _():
            for d in range(last):
                downb_copy(own_b, k, d).start()

    def add_into(dst, src):
        for j in range(tpc):
            dst[j] = (dst[j].astype(F32) + src[j].astype(F32)).astype(BF16)

    def step(i, carry):
        @pl.when(i + AHEAD < na)
        def _():
            send_x(i + AHEAD)

        @pl.when((i % B_EVERY == 0) & (i // B_EVERY < N_B))
        def _():
            send_b(i // B_EVERY)

        @pl.when(i < na)
        def _():
            x_copy(i).wait_recv()

            def one(d, c):
                for j in range(tpc):
                    xrecv[i, d, j] = (part(i, 2 * d + x, j) + xrecv[i, d, j].astype(F32)).astype(BF16)
                return c

            lax.fori_loop(0, n, one, 0)

            @pl.when(z == 0)
            def _():
                for d in range(last, 0, -1):
                    up_copy(xrecv, i, d).start()

            @pl.when(z == last)
            def _():
                for d in range(last):
                    down_copy(xrecv, i, d).start()

        q = i - LAG * z

        @pl.when((z > 0) & (z < last) & (q >= 0) & (q < na))
        def _():
            for d in range(last, 1, -1):
                @pl.when(d > z)
                def _():
                    up_copy(up, q, d).wait_recv()
                    add_into(up.at[q, d], xrecv.at[q, d])
                    up_copy(up, q, d).start()

        w = i - LAG * (last - z)

        @pl.when((z > 0) & (z < last) & (w >= 0) & (w < na))
        def _():
            for d in range(last - 1):
                @pl.when(d < z)
                def _():
                    down_copy(down, w, d).wait_recv()
                    add_into(down.at[w, d], xrecv.at[w, d])
                    down_copy(down, w, d).start()

        f = i - LAG * last

        @pl.when((f >= 0) & (f < na))
        def _():
            @pl.when(z > 0)
            def _():
                up_copy(up, f, z).wait_recv()

            @pl.when(z < last)
            def _():
                down_copy(down, f, z).wait_recv()

            for j in range(tpc):
                total = xrecv[f, z, j].astype(F32)
                total += jnp.where(z > 0, up[f, z, j].astype(F32), 0.0)
                total += jnp.where(z < last, down[f, z, j].astype(F32), 0.0)
                out_ref[f, :, j * tw:(j + 1) * tw] = (total / n_rep).astype(BF16)

        bu = i - B_LAG * z

        @pl.when((z > 0) & (z < last) & (bu >= 0) & (bu % B_EVERY == 0) & (bu // B_EVERY < N_B))
        def _():
            k = bu // B_EVERY
            for d in range(last, 1, -1):
                @pl.when(d > z)
                def _():
                    upb_copy(up_b, k, d).wait_recv()
                    for c in range(2):
                        add_into(up_b.at[k, d, c], own_b.at[k, d, c])
                    upb_copy(up_b, k, d).start()

        bd = i - B_LAG * (last - z)

        @pl.when((z > 0) & (z < last) & (bd >= 0) & (bd % B_EVERY == 0) & (bd // B_EVERY < N_B))
        def _():
            k = bd // B_EVERY
            for d in range(last - 1):
                @pl.when(d < z)
                def _():
                    downb_copy(down_b, k, d).wait_recv()
                    for c in range(2):
                        add_into(down_b.at[k, d, c], own_b.at[k, d, c])
                    downb_copy(down_b, k, d).start()

        bf = i - B_LAG * last

        @pl.when((bf >= 0) & (bf % B_EVERY == 0) & (bf // B_EVERY < N_B))
        def _():
            k = bf // B_EVERY

            @pl.when(z > 0)
            def _():
                upb_copy(up_b, k, z).wait_recv()

            @pl.when(z < last)
            def _():
                downb_copy(down_b, k, z).wait_recv()

            def total(c, j):
                t = own_b[k, z, c, j].astype(F32)
                t += jnp.where(z > 0, up_b[k, z, c, j].astype(F32), 0.0)
                return t + jnp.where(z < last, down_b[k, z, c, j].astype(F32), 0.0)

            for j in range(tpc):
                xs_b[k, j] = total(1 - x, j).astype(BF16)
            xb_copy(k).start()
            for j in range(tpc):
                own_b[k, z, x, j] = total(x, j).astype(BF16)

        return carry

    steps = max(na + LAG * last, B_EVERY * (N_B - 1) + B_LAG * last + 1)
    lax.fori_loop(0, steps, step, 0)

    def finish_b(k, carry):
        xb_copy(k).wait_recv()
        for j in range(tpc):
            total = own_b[k, z, x, j].astype(F32) + xr_b[k, j].astype(F32)
            out_ref[na + k, :, j * tw:(j + 1) * tw] = (total / n_rep).astype(BF16)
        xb_copy(k).wait_send()
        return carry

    lax.fori_loop(0, N_B, finish_b, 0)

    def drain(i, carry):
        x_copy(i).wait_send()

        @pl.when(z < last)
        def _():
            for d in range(1, n):
                @pl.when(d > z)
                def _():
                    up_copy(up, i, d).wait_send()

        @pl.when(z > 0)
        def _():
            for d in range(last):
                @pl.when(d < z)
                def _():
                    down_copy(down, i, d).wait_send()

        return carry

    lax.fori_loop(0, na, drain, 0)

    def drain_b(k, carry):
        @pl.when(z < last)
        def _():
            for d in range(1, n):
                @pl.when(d > z)
                def _():
                    upb_copy(up_b, k, d).wait_send()

        @pl.when(z > 0)
        def _():
            for d in range(last):
                @pl.when(d < z)
                def _():
                    downb_copy(down_b, k, d).wait_send()

        return carry

    lax.fori_loop(0, N_B, drain_b, 0)


def reduce_deltas(left, right, n_rep, columns):
    n = n_rep // 2
    pr, depth = left.shape[2:]
    tw = right.shape[2]
    tpc = columns // tw
    na = PIECES - N_B
    chunk = (tpc, pr, tw)
    dma = pltpu.SemaphoreType.DMA
    vmem = pl.BlockSpec(memory_space=pltpu.VMEM)
    out = pl.pallas_call(
        functools.partial(reduce_kernel, n),
        out_shape=jax.ShapeDtypeStruct((PIECES, pr, columns), BF16),
        in_specs=[vmem] * 2,
        out_specs=vmem,
        scratch_shapes=[
            pltpu.VMEM((na, n) + chunk, BF16),
            pltpu.VMEM((na, n) + chunk, BF16),
            pltpu.VMEM((na, n) + chunk, BF16),
            pltpu.VMEM((na, n) + chunk, BF16),
            pltpu.VMEM((N_B, n, 2) + chunk, BF16),
            pltpu.VMEM((N_B, n, 2) + chunk, BF16),
            pltpu.VMEM((N_B, n, 2) + chunk, BF16),
            pltpu.VMEM((N_B,) + chunk, BF16),
            pltpu.VMEM((N_B,) + chunk, BF16),
            dma((na,)),
            dma((na,)),
            dma((na, n)),
            dma((na, n)),
            dma((na, n)),
            dma((na, n)),
            dma((N_B, n)),
            dma((N_B, n)),
            dma((N_B, n)),
            dma((N_B, n)),
            dma((N_B,)),
            dma((N_B,)),
        ],
        compiler_params=pltpu.CompilerParams(
            collective_id=0, has_side_effects=True, vmem_limit_bytes=56 * 2**20
        ),
        cost_estimate=pl.CostEstimate(
            flops=2 * 3 * PIECES * pr * depth * columns * n_rep // 3,
            bytes_accessed=8 * 2**20, transcendentals=0,
        ),
    )(left, right)
    return out.reshape(PIECES * pr, columns)


def body(tokens, expert_ids, gate_prob, cotangent, w_gate, w_up, w_down, touched):
    rows = tokens.shape[0]
    width = tokens.shape[1]
    n_exp = lax.axis_size("exp")
    n_rep = lax.axis_size("rep")
    shards = n_exp // EW
    cap = rows // EW
    onehot = (expert_ids == jnp.arange(EW)[None, :]).astype(jnp.float32)
    lower = (
        lax.broadcasted_iota(jnp.int32, (rows, rows), 0)
        > lax.broadcasted_iota(jnp.int32, (rows, rows), 1)
    ).astype(jnp.float32)
    earlier = jnp.dot(lower, onehot, precision=lax.Precision.HIGHEST)
    slot_of = jnp.sum(onehot * earlier, axis=1).astype(jnp.int32)
    target = expert_ids[:, 0] * cap + slot_of
    placer = (target[None, :] == jnp.arange(EW * cap)[:, None]).astype(jnp.bfloat16)
    dy = (gate_prob[:, None] * cotangent.astype(jnp.float32)).astype(jnp.bfloat16)
    both = jnp.dot(
        placer, jnp.concatenate([tokens, dy], axis=1), preferred_element_type=jnp.float32
    ).astype(jnp.bfloat16).reshape(EW, cap, 2 * width)
    recv = lax.all_to_all(
        jnp.repeat(both, shards, axis=0), "exp", split_axis=0, concat_axis=0, tiled=True
    ).reshape(n_exp * cap, 2 * width)
    x_rows = recv[:, :width]
    d_rows = recv[:, width:]
    wg = w_gate[0]
    wu = w_up[0]
    wd = w_down[0]
    h = jnp.dot(x_rows, wg, preferred_element_type=jnp.float32)
    u = jnp.dot(x_rows, wu, preferred_element_type=jnp.float32)
    act = (h * jax.nn.sigmoid(h) * u).astype(jnp.bfloat16)
    partial_out = jnp.dot(act, wd, preferred_element_type=jnp.float32).astype(jnp.bfloat16)
    returned = lax.all_to_all(
        partial_out.reshape(n_exp, cap, width), "exp", split_axis=0, concat_axis=0, tiled=True
    )
    summed = returned.astype(jnp.float32).reshape(EW, shards, cap, width).sum(axis=1)
    row_out = jnp.take(summed.reshape(EW * cap, width), target, axis=0)
    mixed = (gate_prob[:, None] * row_out).astype(jnp.bfloat16)
    grad_a = lax.dot_general(
        d_rows, wd, (((1,), (1,)), ((), ())), preferred_element_type=jnp.float32
    )
    d_h = (grad_a * u * swish_slope(h)).astype(jnp.bfloat16)
    d_u = (grad_a * h * jax.nn.sigmoid(h)).astype(jnp.bfloat16)
    hidden = d_h.shape[1]
    columns = 3 * width // n_rep
    tw = math.gcd(columns, width)
    mask = jnp.repeat(touched[0], TILE).astype(jnp.bfloat16)
    left = (jnp.stack([d_h, d_u, act]) * mask[None, None, :]).transpose(0, 2, 1)
    left = left.reshape(3, PIECES, hidden // PIECES, left.shape[2])
    right = recv.reshape(recv.shape[0], 2 * width // tw, tw).transpose(1, 0, 2)
    averaged = reduce_deltas(left, right, n_rep, columns)
    return (mixed, averaged)


def solution(mesh):
    return jax.shard_map(
        body,
        mesh=mesh,
        in_specs=(
            P(("rep", "exp"), None),
            P(("rep", "exp"), None),
            P(("rep", "exp")),
            P(("rep", "exp"), None),
            P("rep", None, "exp"),
            P("rep", None, "exp"),
            P("rep", "exp", None),
            P("rep", "exp"),
        ),
        out_specs=(P(("rep", "exp"), None), P("exp", "rep")),
        check_vma=False,
    )
```

```python
import functools
import math

import jax
import jax.numpy as jnp
from jax import lax
from jax.experimental import pallas as pl
from jax.experimental.pallas import tpu as pltpu
from jax.sharding import PartitionSpec as P

EW = 4
TILE = 16
PIECES = 16
N_B = 3
AHEAD = 3
LAG = 2
B_LAG = 2
B_EVERY = 4
F32 = jnp.float32
BF16 = jnp.bfloat16


def swish_slope(h):
    s = jax.nn.sigmoid(h)
    return s * (1.0 + h * (1.0 - s))


def exp_copy(src, dst, send, recv, dev):
    return pltpu.make_async_remote_copy(
        src_ref=src, dst_ref=dst, send_sem=send, recv_sem=recv,
        device_id={"exp": dev}, device_id_type=pl.DeviceIdType.MESH,
    )


def greet_exp(barrier, n_exp):
    me = lax.axis_index("exp")
    for k in range(1, n_exp):
        pl.semaphore_signal(
            barrier, inc=1, device_id={"exp": (me + k) % n_exp},
            device_id_type=pl.DeviceIdType.MESH,
        )


def exchange_start(n_exp, group, src, land, send_sem, recv_sem):
    me = lax.axis_index("exp")
    for k in range(n_exp - 1, 0, -1):
        to = (me + k) % n_exp
        exp_copy(
            src.at[to // group], land.at[me], send_sem.at[k - 1], recv_sem.at[k - 1], to
        ).start()
    land[me] = src[me // group]


def exchange_wait(n_exp, src, land, send_sem, recv_sem):
    me = lax.axis_index("exp")
    for k in range(n_exp - 1, 0, -1):
        come = (me + n_exp - k) % n_exp
        copy = exp_copy(src.at[0], land.at[come], send_sem.at[k - 1], recv_sem.at[k - 1], come)
        copy.wait_recv()
        copy.wait_send()


def dispatch_kernel(
    n_exp, tok_ref, cot_ref, gate_ref, place_ref, rows_ref, tiles_ref, buf, land, send_sem, recv_sem
):
    width = tok_ref.shape[1]
    tw = tiles_ref.shape[3]
    barrier = pltpu.get_barrier_semaphore()
    greet_exp(barrier, n_exp)
    dy = (gate_ref[...] * cot_ref[...].astype(F32)).astype(BF16)
    for e in range(EW):
        buf[e, :, :width] = jnp.dot(
            place_ref[e], tok_ref[...], preferred_element_type=F32
        ).astype(BF16)
        buf[e, :, width:] = jnp.dot(place_ref[e], dy, preferred_element_type=F32).astype(BF16)
    pl.semaphore_wait(barrier, n_exp - 1)
    exchange_start(n_exp, n_exp // EW, buf, land, send_sem, recv_sem)
    exchange_wait(n_exp, buf, land, send_sem, recv_sem)
    rows_ref[...] = land[...]

    def one(s, c):
        for t in range(2 * width // tw):
            tiles_ref[t, s] = land[s, :, t * tw:(t + 1) * tw]
        return c

    lax.fori_loop(0, n_exp, one, 0)


def dispatch(tokens, cotangent, gate, placer, n_exp, tw):
    rows, width = tokens.shape
    cap = rows // EW
    vmem = pl.BlockSpec(memory_space=pltpu.VMEM)
    return pl.pallas_call(
        functools.partial(dispatch_kernel, n_exp),
        out_shape=(
            jax.ShapeDtypeStruct((n_exp, cap, 2 * width), BF16),
            jax.ShapeDtypeStruct((2 * width // tw, n_exp, cap, tw), BF16),
        ),
        in_specs=[vmem] * 4,
        out_specs=(vmem, vmem),
        scratch_shapes=[
            pltpu.VMEM((EW, cap, 2 * width), BF16),
            pltpu.VMEM((n_exp, cap, 2 * width), BF16),
            pltpu.SemaphoreType.DMA((n_exp - 1,)),
            pltpu.SemaphoreType.DMA((n_exp - 1,)),
        ],
        compiler_params=pltpu.CompilerParams(
            collective_id=1, has_side_effects=True, vmem_limit_bytes=48 * 2**20
        ),
        cost_estimate=pl.CostEstimate(
            flops=4 * rows * rows * width, bytes_accessed=6 * 2**20, transcendentals=0
        ),
    )(tokens, cotangent, gate, placer.reshape(EW, cap, rows))


def reduce_kernel(
    n, n_exp, l_ref, r_ref, p_ref, out_ref, ret_ref, ret, rs_sem, rr_sem, xsend, xrecv, up, down, own_b, up_b, down_b, xs_b, xr_b,
    xs_sem, xr_sem, us_sem, ur_sem, ds_sem, dr_sem,
    bus_sem, bur_sem, bds_sem, bdr_sem, bxs_sem, bxr_sem,
):
    na = PIECES - N_B
    n_rep = 2 * n
    tpc = xsend.shape[2]
    tw = xsend.shape[4]
    pr = xsend.shape[3]
    tpw = r_ref.shape[0] // 2
    rep = lax.axis_index("rep")
    z = rep // 2
    x = rep % 2
    peer = {"rep": rep + 1 - 2 * x}
    above = {"rep": jnp.minimum(rep + 2, n_rep - 1)}
    below = {"rep": jnp.maximum(rep - 2, 0)}
    last = n - 1
    def part(p, r, j):
        t = r * tpc + j
        mat = t // tpw
        src = t % tpw + jnp.where(mat == 2, tpw, 0)
        return jnp.dot(l_ref[mat, p], r_ref[src], preferred_element_type=F32)

    def remote(src, dst, send, recv, dev):
        return pltpu.make_async_remote_copy(
            src_ref=src, dst_ref=dst, send_sem=send, recv_sem=recv,
            device_id=dev, device_id_type=pl.DeviceIdType.MESH,
        )

    def x_copy(p):
        return remote(xsend.at[p], xrecv.at[p], xs_sem.at[p], xr_sem.at[p], peer)

    def up_copy(src, p, d):
        return remote(src.at[p, d], up.at[p, d], us_sem.at[p, d], ur_sem.at[p, d], above)

    def down_copy(src, p, d):
        return remote(src.at[p, d], down.at[p, d], ds_sem.at[p, d], dr_sem.at[p, d], below)

    def upb_copy(src, k, d):
        return remote(src.at[k, d], up_b.at[k, d], bus_sem.at[k, d], bur_sem.at[k, d], above)

    def downb_copy(src, k, d):
        return remote(src.at[k, d], down_b.at[k, d], bds_sem.at[k, d], bdr_sem.at[k, d], below)

    def xb_copy(k):
        return remote(xs_b.at[k], xr_b.at[k], bxs_sem.at[k], bxr_sem.at[k], peer)

    barrier = pltpu.get_barrier_semaphore()
    mesh_id = pl.DeviceIdType.MESH
    greet_exp(barrier, n_exp)
    pl.semaphore_signal(barrier, inc=1, device_id=peer, device_id_type=mesh_id)

    @pl.when(z < last)
    def _():
        pl.semaphore_signal(barrier, inc=1, device_id=above, device_id_type=mesh_id)

    @pl.when(z > 0)
    def _():
        pl.semaphore_signal(barrier, inc=1, device_id=below, device_id_type=mesh_id)

    pl.semaphore_wait(barrier, n_exp + jnp.where(z < last, 1, 0) + jnp.where(z > 0, 1, 0))

    def send_x(p):
        def one(d, c):
            for j in range(tpc):
                xsend[p, d, j] = part(p, 2 * d + 1 - x, j).astype(BF16)
            return c

        lax.fori_loop(0, n, one, 0)
        x_copy(p).start()

    for p in range(AHEAD):
        send_x(p)
    exchange_start(n_exp, 1, p_ref, ret, rs_sem, rr_sem)

    def send_b(k):
        def build_b(r, c):
            for j in range(tpc):
                own_b[k, r // 2, r % 2, j] = part(na + k, r, j).astype(BF16)
            return c

        lax.fori_loop(0, n_rep, build_b, 0)

        @pl.when(z == 0)
        def _():
            for d in range(last, 0, -1):
                upb_copy(own_b, k, d).start()

        @pl.when(z == last)
        def _():
            for d in range(last):
                downb_copy(own_b, k, d).start()

    def add_into(dst, src):
        for j in range(tpc):
            dst[j] = (dst[j].astype(F32) + src[j].astype(F32)).astype(BF16)

    def step(i, carry):
        @pl.when(i + AHEAD < na)
        def _():
            send_x(i + AHEAD)

        @pl.when((i % B_EVERY == 0) & (i // B_EVERY < N_B))
        def _():
            send_b(i // B_EVERY)

        @pl.when(i < na)
        def _():
            x_copy(i).wait_recv()

            def one(d, c):
                for j in range(tpc):
                    xrecv[i, d, j] = (part(i, 2 * d + x, j) + xrecv[i, d, j].astype(F32)).astype(BF16)
                return c

            lax.fori_loop(0, n, one, 0)

            @pl.when(z == 0)
            def _():
                for d in range(last, 0, -1):
                    up_copy(xrecv, i, d).start()

            @pl.when(z == last)
            def _():
                for d in range(last):
                    down_copy(xrecv, i, d).start()

        q = i - LAG * z

        @pl.when((z > 0) & (z < last) & (q >= 0) & (q < na))
        def _():
            for d in range(last, 1, -1):
                @pl.when(d > z)
                def _():
                    up_copy(up, q, d).wait_recv()
                    add_into(up.at[q, d], xrecv.at[q, d])
                    up_copy(up, q, d).start()

        w = i - LAG * (last - z)

        @pl.when((z > 0) & (z < last) & (w >= 0) & (w < na))
        def _():
            for d in range(last - 1):
                @pl.when(d < z)
                def _():
                    down_copy(down, w, d).wait_recv()
                    add_into(down.at[w, d], xrecv.at[w, d])
                    down_copy(down, w, d).start()

        f = i - LAG * last

        @pl.when((f >= 0) & (f < na))
        def _():
            @pl.when(z > 0)
            def _():
                up_copy(up, f, z).wait_recv()

            @pl.when(z < last)
            def _():
                down_copy(down, f, z).wait_recv()

            for j in range(tpc):
                total = xrecv[f, z, j].astype(F32)
                total += jnp.where(z > 0, up[f, z, j].astype(F32), 0.0)
                total += jnp.where(z < last, down[f, z, j].astype(F32), 0.0)
                out_ref[f, :, j * tw:(j + 1) * tw] = (total / n_rep).astype(BF16)

        bu = i - B_LAG * z

        @pl.when((z > 0) & (z < last) & (bu >= 0) & (bu % B_EVERY == 0) & (bu // B_EVERY < N_B))
        def _():
            k = bu // B_EVERY
            for d in range(last, 1, -1):
                @pl.when(d > z)
                def _():
                    upb_copy(up_b, k, d).wait_recv()
                    for c in range(2):
                        add_into(up_b.at[k, d, c], own_b.at[k, d, c])
                    upb_copy(up_b, k, d).start()

        bd = i - B_LAG * (last - z)

        @pl.when((z > 0) & (z < last) & (bd >= 0) & (bd % B_EVERY == 0) & (bd // B_EVERY < N_B))
        def _():
            k = bd // B_EVERY
            for d in range(last - 1):
                @pl.when(d < z)
                def _():
                    downb_copy(down_b, k, d).wait_recv()
                    for c in range(2):
                        add_into(down_b.at[k, d, c], own_b.at[k, d, c])
                    downb_copy(down_b, k, d).start()

        bf = i - B_LAG * last

        @pl.when((bf >= 0) & (bf % B_EVERY == 0) & (bf // B_EVERY < N_B))
        def _():
            k = bf // B_EVERY

            @pl.when(z > 0)
            def _():
                upb_copy(up_b, k, z).wait_recv()

            @pl.when(z < last)
            def _():
                downb_copy(down_b, k, z).wait_recv()

            def total(c, j):
                t = own_b[k, z, c, j].astype(F32)
                t += jnp.where(z > 0, up_b[k, z, c, j].astype(F32), 0.0)
                return t + jnp.where(z < last, down_b[k, z, c, j].astype(F32), 0.0)

            for j in range(tpc):
                xs_b[k, j] = total(1 - x, j).astype(BF16)
            xb_copy(k).start()
            for j in range(tpc):
                own_b[k, z, x, j] = total(x, j).astype(BF16)

        return carry

    steps = max(na + LAG * last, B_EVERY * (N_B - 1) + B_LAG * last + 1)
    lax.fori_loop(0, steps, step, 0)

    exchange_wait(n_exp, p_ref, ret, rs_sem, rr_sem)
    ret_ref[...] = ret[...]

    def finish_b(k, carry):
        xb_copy(k).wait_recv()
        for j in range(tpc):
            total = own_b[k, z, x, j].astype(F32) + xr_b[k, j].astype(F32)
            out_ref[na + k, :, j * tw:(j + 1) * tw] = (total / n_rep).astype(BF16)
        xb_copy(k).wait_send()
        return carry

    lax.fori_loop(0, N_B, finish_b, 0)

    def drain(i, carry):
        x_copy(i).wait_send()

        @pl.when(z < last)
        def _():
            for d in range(1, n):
                @pl.when(d > z)
                def _():
                    up_copy(up, i, d).wait_send()

        @pl.when(z > 0)
        def _():
            for d in range(last):
                @pl.when(d < z)
                def _():
                    down_copy(down, i, d).wait_send()

        return carry

    lax.fori_loop(0, na, drain, 0)

    def drain_b(k, carry):
        @pl.when(z < last)
        def _():
            for d in range(1, n):
                @pl.when(d > z)
                def _():
                    upb_copy(up_b, k, d).wait_send()

        @pl.when(z > 0)
        def _():
            for d in range(last):
                @pl.when(d < z)
                def _():
                    downb_copy(down_b, k, d).wait_send()

        return carry

    lax.fori_loop(0, N_B, drain_b, 0)


def reduce_deltas(left, right, parts, n_rep, columns):
    n = n_rep // 2
    pr, depth = left.shape[2:]
    tw = right.shape[2]
    tpc = columns // tw
    na = PIECES - N_B
    chunk = (tpc, pr, tw)
    dma = pltpu.SemaphoreType.DMA
    vmem = pl.BlockSpec(memory_space=pltpu.VMEM)
    n_exp = parts.shape[0]
    out, returned = pl.pallas_call(
        functools.partial(reduce_kernel, n, n_exp),
        out_shape=(
            jax.ShapeDtypeStruct((PIECES, pr, columns), BF16),
            jax.ShapeDtypeStruct(parts.shape, BF16),
        ),
        in_specs=[vmem] * 3,
        out_specs=(vmem, vmem),
        scratch_shapes=[
            pltpu.VMEM(parts.shape, BF16),
            dma((n_exp - 1,)),
            dma((n_exp - 1,)),
            pltpu.VMEM((na, n) + chunk, BF16),
            pltpu.VMEM((na, n) + chunk, BF16),
            pltpu.VMEM((na, n) + chunk, BF16),
            pltpu.VMEM((na, n) + chunk, BF16),
            pltpu.VMEM((N_B, n, 2) + chunk, BF16),
            pltpu.VMEM((N_B, n, 2) + chunk, BF16),
            pltpu.VMEM((N_B, n, 2) + chunk, BF16),
            pltpu.VMEM((N_B,) + chunk, BF16),
            pltpu.VMEM((N_B,) + chunk, BF16),
            dma((na,)),
            dma((na,)),
            dma((na, n)),
            dma((na, n)),
            dma((na, n)),
            dma((na, n)),
            dma((N_B, n)),
            dma((N_B, n)),
            dma((N_B, n)),
            dma((N_B, n)),
            dma((N_B,)),
            dma((N_B,)),
        ],
        compiler_params=pltpu.CompilerParams(
            collective_id=0, has_side_effects=True, vmem_limit_bytes=56 * 2**20
        ),
        cost_estimate=pl.CostEstimate(
            flops=2 * 3 * PIECES * pr * depth * columns * n_rep // 3,
            bytes_accessed=8 * 2**20, transcendentals=0,
        ),
    )(left, right, parts)
    return out.reshape(PIECES * pr, columns), returned


def body(tokens, expert_ids, gate_prob, cotangent, w_gate, w_up, w_down, touched):
    rows = tokens.shape[0]
    width = tokens.shape[1]
    n_exp = lax.axis_size("exp")
    n_rep = lax.axis_size("rep")
    shards = n_exp // EW
    cap = rows // EW
    onehot = (expert_ids == jnp.arange(EW)[None, :]).astype(jnp.float32)
    lower = (
        lax.broadcasted_iota(jnp.int32, (rows, rows), 0)
        > lax.broadcasted_iota(jnp.int32, (rows, rows), 1)
    ).astype(jnp.float32)
    earlier = jnp.dot(lower, onehot, precision=lax.Precision.HIGHEST)
    slot_of = jnp.sum(onehot * earlier, axis=1).astype(jnp.int32)
    target = expert_ids[:, 0] * cap + slot_of
    placer = (target[None, :] == jnp.arange(EW * cap)[:, None]).astype(jnp.bfloat16)
    columns = 3 * width // n_rep
    tw = math.gcd(columns, width)
    recv, right = dispatch(tokens, cotangent, gate_prob[:, None], placer, n_exp, tw)
    recv = recv.reshape(n_exp * cap, 2 * width)
    right = right.reshape(2 * width // tw, n_exp * cap, tw)
    x_rows = recv[:, :width]
    d_rows = recv[:, width:]
    wg = w_gate[0]
    wu = w_up[0]
    wd = w_down[0]
    h = jnp.dot(x_rows, wg, preferred_element_type=jnp.float32)
    u = jnp.dot(x_rows, wu, preferred_element_type=jnp.float32)
    act = (h * jax.nn.sigmoid(h) * u).astype(jnp.bfloat16)
    partial_out = jnp.dot(act, wd, preferred_element_type=jnp.float32).astype(jnp.bfloat16)
    grad_a = lax.dot_general(
        d_rows, wd, (((1,), (1,)), ((), ())), preferred_element_type=jnp.float32
    )
    d_h = (grad_a * u * swish_slope(h)).astype(jnp.bfloat16)
    d_u = (grad_a * h * jax.nn.sigmoid(h)).astype(jnp.bfloat16)
    hidden = d_h.shape[1]
    mask = jnp.repeat(touched[0], TILE).astype(jnp.bfloat16)
    left = (jnp.stack([d_h, d_u, act]) * mask[None, None, :]).transpose(0, 2, 1)
    left = left.reshape(3, PIECES, hidden // PIECES, left.shape[2])
    averaged, returned = reduce_deltas(
        left, right, partial_out.reshape(n_exp, cap, width), n_rep, columns
    )
    summed = returned.astype(jnp.float32).reshape(EW, shards, cap, width).sum(axis=1)
    row_out = jnp.take(summed.reshape(EW * cap, width), target, axis=0)
    mixed = (gate_prob[:, None] * row_out).astype(jnp.bfloat16)
    return (mixed, averaged)


def solution(mesh):
    return jax.shard_map(
        body,
        mesh=mesh,
        in_specs=(
            P(("rep", "exp"), None),
            P(("rep", "exp"), None),
            P(("rep", "exp")),
            P(("rep", "exp"), None),
            P("rep", None, "exp"),
            P("rep", None, "exp"),
            P("rep", "exp", None),
            P("rep", "exp"),
        ),
        out_specs=(P(("rep", "exp"), None), P("exp", "rep")),
        check_vma=False,
    )
```

```python
import functools
import math

import jax
import jax.numpy as jnp
from jax import lax
from jax.experimental import pallas as pl
from jax.experimental.pallas import tpu as pltpu
from jax.sharding import PartitionSpec as P

EW = 4
TILE = 16
PIECES = 16
N_B = 3
AHEAD = 3
LAG = 2
B_LAG = 2
B_EVERY = 4
F32 = jnp.float32
BF16 = jnp.bfloat16


def swish_slope(h):
    s = jax.nn.sigmoid(h)
    return s * (1.0 + h * (1.0 - s))


def exp_copy(src, dst, send, recv, dev):
    return pltpu.make_async_remote_copy(
        src_ref=src, dst_ref=dst, send_sem=send, recv_sem=recv,
        device_id={"exp": dev}, device_id_type=pl.DeviceIdType.MESH,
    )


def greet_exp(barrier, n_exp):
    me = lax.axis_index("exp")
    for k in range(1, n_exp):
        pl.semaphore_signal(
            barrier, inc=1, device_id={"exp": (me + k) % n_exp},
            device_id_type=pl.DeviceIdType.MESH,
        )


def exchange_start(n_exp, group, src, land, send_sem, recv_sem):
    me = lax.axis_index("exp")
    for k in range(n_exp - 1, 0, -1):
        to = (me + k) % n_exp
        exp_copy(
            src.at[to // group], land.at[me], send_sem.at[k - 1], recv_sem.at[k - 1], to
        ).start()
    land[me] = src[me // group]


def exchange_wait(n_exp, src, land, send_sem, recv_sem):
    me = lax.axis_index("exp")
    for k in range(n_exp - 1, 0, -1):
        come = (me + n_exp - k) % n_exp
        copy = exp_copy(src.at[0], land.at[come], send_sem.at[k - 1], recv_sem.at[k - 1], come)
        copy.wait_recv()
        copy.wait_send()


def dispatch_kernel(
    n_exp, tok_ref, cot_ref, gate_ref, place_ref, rows_ref, tiles_ref, buf, land, send_sem, recv_sem
):
    width = tok_ref.shape[1]
    tw = tiles_ref.shape[3]
    barrier = pltpu.get_barrier_semaphore()
    greet_exp(barrier, n_exp)
    dy = (gate_ref[...] * cot_ref[...].astype(F32)).astype(BF16)
    for e in range(EW):
        buf[e, :, :width] = jnp.dot(
            place_ref[e], tok_ref[...], preferred_element_type=F32
        ).astype(BF16)
        buf[e, :, width:] = jnp.dot(place_ref[e], dy, preferred_element_type=F32).astype(BF16)
    pl.semaphore_wait(barrier, n_exp - 1)
    exchange_start(n_exp, n_exp // EW, buf, land, send_sem, recv_sem)
    exchange_wait(n_exp, buf, land, send_sem, recv_sem)
    rows_ref[...] = land[...]

    def one(s, c):
        for t in range(2 * width // tw):
            tiles_ref[t, s] = land[s, :, t * tw:(t + 1) * tw]
        return c

    lax.fori_loop(0, n_exp, one, 0)


def dispatch(tokens, cotangent, gate, placer, n_exp, tw):
    rows, width = tokens.shape
    cap = rows // EW
    vmem = pl.BlockSpec(memory_space=pltpu.VMEM)
    return pl.pallas_call(
        functools.partial(dispatch_kernel, n_exp),
        out_shape=(
            jax.ShapeDtypeStruct((n_exp, cap, 2 * width), BF16),
            jax.ShapeDtypeStruct((2 * width // tw, n_exp, cap, tw), BF16),
        ),
        in_specs=[vmem] * 4,
        out_specs=(vmem, vmem),
        scratch_shapes=[
            pltpu.VMEM((EW, cap, 2 * width), BF16),
            pltpu.VMEM((n_exp, cap, 2 * width), BF16),
            pltpu.SemaphoreType.DMA((n_exp - 1,)),
            pltpu.SemaphoreType.DMA((n_exp - 1,)),
        ],
        compiler_params=pltpu.CompilerParams(
            collective_id=1, has_side_effects=True, vmem_limit_bytes=48 * 2**20
        ),
        cost_estimate=pl.CostEstimate(
            flops=4 * rows * rows * width, bytes_accessed=6 * 2**20, transcendentals=0
        ),
    )(tokens, cotangent, gate, placer.reshape(EW, cap, rows))


def reduce_kernel(
    n, n_exp, l_ref, r_ref, p_ref, home_ref, gate_ref, out_ref, mix_ref, ret, rs_sem, rr_sem, xsend, xrecv, up, down, own_b, up_b, down_b, xs_b, xr_b,
    xs_sem, xr_sem, us_sem, ur_sem, ds_sem, dr_sem,
    bus_sem, bur_sem, bds_sem, bdr_sem, bxs_sem, bxr_sem,
):
    na = PIECES - N_B
    n_rep = 2 * n
    tpc = xsend.shape[2]
    tw = xsend.shape[4]
    pr = xsend.shape[3]
    tpw = r_ref.shape[0] // 2
    rep = lax.axis_index("rep")
    z = rep // 2
    x = rep % 2
    peer = {"rep": rep + 1 - 2 * x}
    above = {"rep": jnp.minimum(rep + 2, n_rep - 1)}
    below = {"rep": jnp.maximum(rep - 2, 0)}
    last = n - 1
    def part(p, r, j):
        t = r * tpc + j
        mat = t // tpw
        src = t % tpw + jnp.where(mat == 2, tpw, 0)
        return jnp.dot(l_ref[mat, p], r_ref[src], preferred_element_type=F32)

    def remote(src, dst, send, recv, dev):
        return pltpu.make_async_remote_copy(
            src_ref=src, dst_ref=dst, send_sem=send, recv_sem=recv,
            device_id=dev, device_id_type=pl.DeviceIdType.MESH,
        )

    def x_copy(p):
        return remote(xsend.at[p], xrecv.at[p], xs_sem.at[p], xr_sem.at[p], peer)

    def up_copy(src, p, d):
        return remote(src.at[p, d], up.at[p, d], us_sem.at[p, d], ur_sem.at[p, d], above)

    def down_copy(src, p, d):
        return remote(src.at[p, d], down.at[p, d], ds_sem.at[p, d], dr_sem.at[p, d], below)

    def upb_copy(src, k, d):
        return remote(src.at[k, d], up_b.at[k, d], bus_sem.at[k, d], bur_sem.at[k, d], above)

    def downb_copy(src, k, d):
        return remote(src.at[k, d], down_b.at[k, d], bds_sem.at[k, d], bdr_sem.at[k, d], below)

    def xb_copy(k):
        return remote(xs_b.at[k], xr_b.at[k], bxs_sem.at[k], bxr_sem.at[k], peer)

    barrier = pltpu.get_barrier_semaphore()
    mesh_id = pl.DeviceIdType.MESH
    greet_exp(barrier, n_exp)
    pl.semaphore_signal(barrier, inc=1, device_id=peer, device_id_type=mesh_id)

    @pl.when(z < last)
    def _():
        pl.semaphore_signal(barrier, inc=1, device_id=above, device_id_type=mesh_id)

    @pl.when(z > 0)
    def _():
        pl.semaphore_signal(barrier, inc=1, device_id=below, device_id_type=mesh_id)

    pl.semaphore_wait(barrier, n_exp + jnp.where(z < last, 1, 0) + jnp.where(z > 0, 1, 0))

    def send_x(p):
        def one(d, c):
            for j in range(tpc):
                xsend[p, d, j] = part(p, 2 * d + 1 - x, j).astype(BF16)
            return c

        lax.fori_loop(0, n, one, 0)
        x_copy(p).start()

    def send_b(k):
        def one(m, c):
            d = jnp.where(z == 0, last - m, m)

            def build(xi, c):
                for j in range(tpc):
                    own_b[k, d, xi, j] = part(na + k, 2 * d + xi, j).astype(BF16)
                return c

            lax.fori_loop(0, 2, build, 0)

            @pl.when((z == 0) & (m < last))
            def _():
                upb_copy(own_b, k, d).start()

            @pl.when((z == last) & (m < last))
            def _():
                downb_copy(own_b, k, d).start()

            return c

        lax.fori_loop(0, n, one, 0)

    send_b(0)
    for p in range(AHEAD):
        send_x(p)
    exchange_start(n_exp, 1, p_ref, ret, rs_sem, rr_sem)

    def add_into(dst, src):
        for j in range(tpc):
            dst[j] = (dst[j].astype(F32) + src[j].astype(F32)).astype(BF16)

    def combine():
        width = ret.shape[2]
        cw = math.gcd(width, 512)
        for c in range(0, width, cw):
            rows = jnp.zeros((mix_ref.shape[0], cw), F32)
            for s in range(n_exp):
                rows += jnp.dot(
                    home_ref[s * EW // n_exp], ret[s, :, c:c + cw], preferred_element_type=F32
                )
            mix_ref[:, c:c + cw] = (gate_ref[...] * rows).astype(BF16)

    def step(i, carry):
        @pl.when(i == na)
        def _():
            exchange_wait(n_exp, p_ref, ret, rs_sem, rr_sem)
            combine()

        @pl.when(i + AHEAD < na)
        def _():
            send_x(i + AHEAD)

        @pl.when((i > 0) & (i % B_EVERY == 0) & (i // B_EVERY < N_B))
        def _():
            send_b(i // B_EVERY)

        @pl.when(i < na)
        def _():
            x_copy(i).wait_recv()

            def one(d, c):
                for j in range(tpc):
                    xrecv[i, d, j] = (part(i, 2 * d + x, j) + xrecv[i, d, j].astype(F32)).astype(BF16)
                return c

            lax.fori_loop(0, n, one, 0)

            @pl.when(z == 0)
            def _():
                for d in range(last, 0, -1):
                    up_copy(xrecv, i, d).start()

            @pl.when(z == last)
            def _():
                for d in range(last):
                    down_copy(xrecv, i, d).start()

        q = i - LAG * z

        @pl.when((z > 0) & (z < last) & (q >= 0) & (q < na))
        def _():
            for d in range(last, 1, -1):
                @pl.when(d > z)
                def _():
                    up_copy(up, q, d).wait_recv()
                    add_into(up.at[q, d], xrecv.at[q, d])
                    up_copy(up, q, d).start()

        w = i - LAG * (last - z)

        @pl.when((z > 0) & (z < last) & (w >= 0) & (w < na))
        def _():
            for d in range(last - 1):
                @pl.when(d < z)
                def _():
                    down_copy(down, w, d).wait_recv()
                    add_into(down.at[w, d], xrecv.at[w, d])
                    down_copy(down, w, d).start()

        f = i - LAG * last

        @pl.when((f >= 0) & (f < na))
        def _():
            @pl.when(z > 0)
            def _():
                up_copy(up, f, z).wait_recv()

            @pl.when(z < last)
            def _():
                down_copy(down, f, z).wait_recv()

            for j in range(tpc):
                total = xrecv[f, z, j].astype(F32)
                total += jnp.where(z > 0, up[f, z, j].astype(F32), 0.0)
                total += jnp.where(z < last, down[f, z, j].astype(F32), 0.0)
                out_ref[f, :, j * tw:(j + 1) * tw] = (total / n_rep).astype(BF16)

        bu = i - B_LAG * z

        @pl.when((z > 0) & (z < last) & (bu >= 0) & (bu % B_EVERY == 0) & (bu // B_EVERY < N_B))
        def _():
            k = bu // B_EVERY
            for d in range(last, 1, -1):
                @pl.when(d > z)
                def _():
                    upb_copy(up_b, k, d).wait_recv()
                    for c in range(2):
                        add_into(up_b.at[k, d, c], own_b.at[k, d, c])
                    upb_copy(up_b, k, d).start()

        bd = i - B_LAG * (last - z)

        @pl.when((z > 0) & (z < last) & (bd >= 0) & (bd % B_EVERY == 0) & (bd // B_EVERY < N_B))
        def _():
            k = bd // B_EVERY
            for d in range(last - 1):
                @pl.when(d < z)
                def _():
                    downb_copy(down_b, k, d).wait_recv()
                    for c in range(2):
                        add_into(down_b.at[k, d, c], own_b.at[k, d, c])
                    downb_copy(down_b, k, d).start()

        bf = i - B_LAG * last

        @pl.when((bf >= 0) & (bf % B_EVERY == 0) & (bf // B_EVERY < N_B))
        def _():
            k = bf // B_EVERY

            @pl.when(z > 0)
            def _():
                upb_copy(up_b, k, z).wait_recv()

            @pl.when(z < last)
            def _():
                downb_copy(down_b, k, z).wait_recv()

            def total(c, j):
                t = own_b[k, z, c, j].astype(F32)
                t += jnp.where(z > 0, up_b[k, z, c, j].astype(F32), 0.0)
                return t + jnp.where(z < last, down_b[k, z, c, j].astype(F32), 0.0)

            for j in range(tpc):
                xs_b[k, j] = total(1 - x, j).astype(BF16)
            xb_copy(k).start()
            for j in range(tpc):
                own_b[k, z, x, j] = total(x, j).astype(BF16)

        return carry

    steps = max(na + LAG * last, B_EVERY * (N_B - 1) + B_LAG * last + 1)
    lax.fori_loop(0, steps, step, 0)

    def finish_b(k, carry):
        xb_copy(k).wait_recv()
        for j in range(tpc):
            total = own_b[k, z, x, j].astype(F32) + xr_b[k, j].astype(F32)
            out_ref[na + k, :, j * tw:(j + 1) * tw] = (total / n_rep).astype(BF16)
        xb_copy(k).wait_send()
        return carry

    lax.fori_loop(0, N_B, finish_b, 0)

    def drain(i, carry):
        x_copy(i).wait_send()

        @pl.when(z < last)
        def _():
            for d in range(1, n):
                @pl.when(d > z)
                def _():
                    up_copy(up, i, d).wait_send()

        @pl.when(z > 0)
        def _():
            for d in range(last):
                @pl.when(d < z)
                def _():
                    down_copy(down, i, d).wait_send()

        return carry

    lax.fori_loop(0, na, drain, 0)

    def drain_b(k, carry):
        @pl.when(z < last)
        def _():
            for d in range(1, n):
                @pl.when(d > z)
                def _():
                    upb_copy(up_b, k, d).wait_send()

        @pl.when(z > 0)
        def _():
            for d in range(last):
                @pl.when(d < z)
                def _():
                    downb_copy(down_b, k, d).wait_send()

        return carry

    lax.fori_loop(0, N_B, drain_b, 0)


def reduce_deltas(left, right, parts, home, gate, n_rep, columns):
    n = n_rep // 2
    pr, depth = left.shape[2:]
    tw = right.shape[2]
    tpc = columns // tw
    na = PIECES - N_B
    chunk = (tpc, pr, tw)
    dma = pltpu.SemaphoreType.DMA
    vmem = pl.BlockSpec(memory_space=pltpu.VMEM)
    n_exp = parts.shape[0]
    out, mixed = pl.pallas_call(
        functools.partial(reduce_kernel, n, n_exp),
        out_shape=(
            jax.ShapeDtypeStruct((PIECES, pr, columns), BF16),
            jax.ShapeDtypeStruct((gate.shape[0], parts.shape[2]), BF16),
        ),
        in_specs=[vmem] * 5,
        out_specs=(vmem, vmem),
        scratch_shapes=[
            pltpu.VMEM(parts.shape, BF16),
            dma((n_exp - 1,)),
            dma((n_exp - 1,)),
            pltpu.VMEM((na, n) + chunk, BF16),
            pltpu.VMEM((na, n) + chunk, BF16),
            pltpu.VMEM((na, n) + chunk, BF16),
            pltpu.VMEM((na, n) + chunk, BF16),
            pltpu.VMEM((N_B, n, 2) + chunk, BF16),
            pltpu.VMEM((N_B, n, 2) + chunk, BF16),
            pltpu.VMEM((N_B, n, 2) + chunk, BF16),
            pltpu.VMEM((N_B,) + chunk, BF16),
            pltpu.VMEM((N_B,) + chunk, BF16),
            dma((na,)),
            dma((na,)),
            dma((na, n)),
            dma((na, n)),
            dma((na, n)),
            dma((na, n)),
            dma((N_B, n)),
            dma((N_B, n)),
            dma((N_B, n)),
            dma((N_B, n)),
            dma((N_B,)),
            dma((N_B,)),
        ],
        compiler_params=pltpu.CompilerParams(
            collective_id=0, has_side_effects=True, vmem_limit_bytes=56 * 2**20
        ),
        cost_estimate=pl.CostEstimate(
            flops=2 * 3 * PIECES * pr * depth * columns * n_rep // 3,
            bytes_accessed=8 * 2**20, transcendentals=0,
        ),
    )(left, right, parts, home, gate)
    return out.reshape(PIECES * pr, columns), mixed


def body(tokens, expert_ids, gate_prob, cotangent, w_gate, w_up, w_down, touched):
    rows = tokens.shape[0]
    width = tokens.shape[1]
    n_exp = lax.axis_size("exp")
    n_rep = lax.axis_size("rep")
    cap = rows // EW
    onehot = (expert_ids == jnp.arange(EW)[None, :]).astype(jnp.float32)
    lower = (
        lax.broadcasted_iota(jnp.int32, (rows, rows), 0)
        > lax.broadcasted_iota(jnp.int32, (rows, rows), 1)
    ).astype(jnp.float32)
    earlier = jnp.dot(lower, onehot, precision=lax.Precision.HIGHEST)
    slot_of = jnp.sum(onehot * earlier, axis=1).astype(jnp.int32)
    target = expert_ids[:, 0] * cap + slot_of
    placer = (target[None, :] == jnp.arange(EW * cap)[:, None]).astype(jnp.bfloat16)
    columns = 3 * width // n_rep
    tw = math.gcd(columns, width)
    recv, right = dispatch(tokens, cotangent, gate_prob[:, None], placer, n_exp, tw)
    recv = recv.reshape(n_exp * cap, 2 * width)
    right = right.reshape(2 * width // tw, n_exp * cap, tw)
    x_rows = recv[:, :width]
    d_rows = recv[:, width:]
    wg = w_gate[0]
    wu = w_up[0]
    wd = w_down[0]
    h = jnp.dot(x_rows, wg, preferred_element_type=jnp.float32)
    u = jnp.dot(x_rows, wu, preferred_element_type=jnp.float32)
    act = (h * jax.nn.sigmoid(h) * u).astype(jnp.bfloat16)
    partial_out = jnp.dot(act, wd, preferred_element_type=jnp.float32).astype(jnp.bfloat16)
    grad_a = lax.dot_general(
        d_rows, wd, (((1,), (1,)), ((), ())), preferred_element_type=jnp.float32
    )
    d_h = (grad_a * u * swish_slope(h)).astype(jnp.bfloat16)
    d_u = (grad_a * h * jax.nn.sigmoid(h)).astype(jnp.bfloat16)
    hidden = d_h.shape[1]
    mask = jnp.repeat(touched[0], TILE).astype(jnp.bfloat16)
    left = (jnp.stack([d_h, d_u, act]) * mask[None, None, :]).transpose(0, 2, 1)
    left = left.reshape(3, PIECES, hidden // PIECES, left.shape[2])
    home = (
        target[None, :, None] == jnp.arange(EW * cap).reshape(EW, 1, cap)
    ).astype(jnp.bfloat16)
    averaged, mixed = reduce_deltas(
        left, right, partial_out.reshape(n_exp, cap, width), home, gate_prob[:, None],
        n_rep, columns,
    )
    return (mixed, averaged)


def solution(mesh):
    return jax.shard_map(
        body,
        mesh=mesh,
        in_specs=(
            P(("rep", "exp"), None),
            P(("rep", "exp"), None),
            P(("rep", "exp")),
            P(("rep", "exp"), None),
            P("rep", None, "exp"),
            P("rep", None, "exp"),
            P("rep", "exp", None),
            P("rep", "exp"),
        ),
        out_specs=(P(("rep", "exp"), None), P("exp", "rep")),
        check_vma=False,
    )
```

```python
import functools
import math

import jax
import jax.numpy as jnp
from jax import lax
from jax.experimental import pallas as pl
from jax.experimental.pallas import tpu as pltpu
from jax.sharding import PartitionSpec as P

EW = 4
TILE = 16
PIECES = 16
N_B = 3
AHEAD = 4
LAG = 2
B_LAG = 2
B_EVERY = 4
F32 = jnp.float32
BF16 = jnp.bfloat16


def swish_slope(h):
    s = jax.nn.sigmoid(h)
    return s * (1.0 + h * (1.0 - s))


def exp_copy(src, dst, send, recv, dev):
    return pltpu.make_async_remote_copy(
        src_ref=src, dst_ref=dst, send_sem=send, recv_sem=recv,
        device_id={"exp": dev}, device_id_type=pl.DeviceIdType.MESH,
    )


def greet_exp(barrier, n_exp):
    me = lax.axis_index("exp")
    for k in range(1, n_exp):
        pl.semaphore_signal(
            barrier, inc=1, device_id={"exp": (me + k) % n_exp},
            device_id_type=pl.DeviceIdType.MESH,
        )


def exchange_start(n_exp, group, src, land, send_sem, recv_sem):
    me = lax.axis_index("exp")
    for k in range(n_exp - 1, 0, -1):
        to = (me + k) % n_exp
        exp_copy(
            src.at[to // group], land.at[me], send_sem.at[k - 1], recv_sem.at[k - 1], to
        ).start()
    land[me] = src[me // group]


def exchange_wait(n_exp, src, land, send_sem, recv_sem):
    me = lax.axis_index("exp")
    for k in range(n_exp - 1, 0, -1):
        come = (me + n_exp - k) % n_exp
        copy = exp_copy(src.at[0], land.at[come], send_sem.at[k - 1], recv_sem.at[k - 1], come)
        copy.wait_recv()
        copy.wait_send()


def dispatch_kernel(
    n_exp, tok_ref, cot_ref, gate_ref, place_ref, rows_ref, tiles_ref, buf, land, send_sem, recv_sem
):
    width = tok_ref.shape[1]
    tw = tiles_ref.shape[3]
    barrier = pltpu.get_barrier_semaphore()
    greet_exp(barrier, n_exp)
    dy = (gate_ref[...] * cot_ref[...].astype(F32)).astype(BF16)
    for e in range(EW):
        buf[e, :, :width] = jnp.dot(
            place_ref[e], tok_ref[...], preferred_element_type=F32
        ).astype(BF16)
        buf[e, :, width:] = jnp.dot(place_ref[e], dy, preferred_element_type=F32).astype(BF16)
    pl.semaphore_wait(barrier, n_exp - 1)
    exchange_start(n_exp, n_exp // EW, buf, land, send_sem, recv_sem)
    exchange_wait(n_exp, buf, land, send_sem, recv_sem)
    rows_ref[...] = land[...]

    def one(s, c):
        for t in range(2 * width // tw):
            tiles_ref[t, s] = land[s, :, t * tw:(t + 1) * tw]
        return c

    lax.fori_loop(0, n_exp, one, 0)


def dispatch(tokens, cotangent, gate, placer, n_exp, tw):
    rows, width = tokens.shape
    cap = rows // EW
    vmem = pl.BlockSpec(memory_space=pltpu.VMEM)
    return pl.pallas_call(
        functools.partial(dispatch_kernel, n_exp),
        out_shape=(
            jax.ShapeDtypeStruct((n_exp, cap, 2 * width), BF16),
            jax.ShapeDtypeStruct((2 * width // tw, n_exp, cap, tw), BF16),
        ),
        in_specs=[vmem] * 4,
        out_specs=(vmem, vmem),
        scratch_shapes=[
            pltpu.VMEM((EW, cap, 2 * width), BF16),
            pltpu.VMEM((n_exp, cap, 2 * width), BF16),
            pltpu.SemaphoreType.DMA((n_exp - 1,)),
            pltpu.SemaphoreType.DMA((n_exp - 1,)),
        ],
        compiler_params=pltpu.CompilerParams(
            collective_id=1, has_side_effects=True, vmem_limit_bytes=48 * 2**20
        ),
        cost_estimate=pl.CostEstimate(
            flops=4 * rows * rows * width, bytes_accessed=6 * 2**20, transcendentals=0
        ),
    )(tokens, cotangent, gate, placer.reshape(EW, cap, rows))


def reduce_kernel(
    n, n_exp, l_ref, r_ref, p_ref, home_ref, gate_ref, out_ref, mix_ref, ret, rs_sem, rr_sem, xsend, xrecv, up, down, own_b, up_b, down_b, xs_b, xr_b,
    xs_sem, xr_sem, us_sem, ur_sem, ds_sem, dr_sem,
    bus_sem, bur_sem, bds_sem, bdr_sem, bxs_sem, bxr_sem,
):
    na = PIECES - N_B
    n_rep = 2 * n
    tpc = xsend.shape[2]
    tw = xsend.shape[4]
    pr = xsend.shape[3]
    tpw = r_ref.shape[0] // 2
    rep = lax.axis_index("rep")
    z = rep // 2
    x = rep % 2
    peer = {"rep": rep + 1 - 2 * x}
    above = {"rep": jnp.minimum(rep + 2, n_rep - 1)}
    below = {"rep": jnp.maximum(rep - 2, 0)}
    last = n - 1
    def part(p, r, j):
        t = r * tpc + j
        mat = t // tpw
        src = t % tpw + jnp.where(mat == 2, tpw, 0)
        return jnp.dot(l_ref[mat, p], r_ref[src], preferred_element_type=F32)

    def remote(src, dst, send, recv, dev):
        return pltpu.make_async_remote_copy(
            src_ref=src, dst_ref=dst, send_sem=send, recv_sem=recv,
            device_id=dev, device_id_type=pl.DeviceIdType.MESH,
        )

    def x_copy(p):
        return remote(xsend.at[p], xrecv.at[p], xs_sem.at[p], xr_sem.at[p], peer)

    def up_copy(src, p, d):
        return remote(src.at[p, d], up.at[p, d], us_sem.at[p, d], ur_sem.at[p, d], above)

    def down_copy(src, p, d):
        return remote(src.at[p, d], down.at[p, d], ds_sem.at[p, d], dr_sem.at[p, d], below)

    def upb_copy(src, k, d):
        return remote(src.at[k, d], up_b.at[k, d], bus_sem.at[k, d], bur_sem.at[k, d], above)

    def downb_copy(src, k, d):
        return remote(src.at[k, d], down_b.at[k, d], bds_sem.at[k, d], bdr_sem.at[k, d], below)

    def xb_copy(k):
        return remote(xs_b.at[k], xr_b.at[k], bxs_sem.at[k], bxr_sem.at[k], peer)

    barrier = pltpu.get_barrier_semaphore()
    mesh_id = pl.DeviceIdType.MESH
    greet_exp(barrier, n_exp)
    pl.semaphore_signal(barrier, inc=1, device_id=peer, device_id_type=mesh_id)

    @pl.when(z < last)
    def _():
        pl.semaphore_signal(barrier, inc=1, device_id=above, device_id_type=mesh_id)

    @pl.when(z > 0)
    def _():
        pl.semaphore_signal(barrier, inc=1, device_id=below, device_id_type=mesh_id)

    pl.semaphore_wait(barrier, n_exp + jnp.where(z < last, 1, 0) + jnp.where(z > 0, 1, 0))

    def send_x(p):
        def one(d, c):
            for j in range(tpc):
                xsend[p, d, j] = part(p, 2 * d + 1 - x, j).astype(BF16)
            return c

        lax.fori_loop(0, n, one, 0)
        x_copy(p).start()

    def send_b(k):
        def one(m, c):
            d = jnp.where(z == 0, last - m, m)

            def build(xi, c):
                for j in range(tpc):
                    own_b[k, d, xi, j] = part(na + k, 2 * d + xi, j).astype(BF16)
                return c

            lax.fori_loop(0, 2, build, 0)

            @pl.when((z == 0) & (m < last))
            def _():
                upb_copy(own_b, k, d).start()

            @pl.when((z == last) & (m < last))
            def _():
                downb_copy(own_b, k, d).start()

            return c

        lax.fori_loop(0, n, one, 0)

    send_x(0)
    send_b(0)
    for p in range(1, AHEAD):
        send_x(p)
    exchange_start(n_exp, 1, p_ref, ret, rs_sem, rr_sem)

    def add_into(dst, src):
        for j in range(tpc):
            dst[j] = (dst[j].astype(F32) + src[j].astype(F32)).astype(BF16)

    def combine():
        width = ret.shape[2]
        cw = math.gcd(width, 512)
        for c in range(0, width, cw):
            rows = jnp.zeros((mix_ref.shape[0], cw), F32)
            for s in range(n_exp):
                rows += jnp.dot(
                    home_ref[s * EW // n_exp], ret[s, :, c:c + cw], preferred_element_type=F32
                )
            mix_ref[:, c:c + cw] = (gate_ref[...] * rows).astype(BF16)

    def step(i, carry):
        @pl.when(i == na // 2)
        def _():
            exchange_wait(n_exp, p_ref, ret, rs_sem, rr_sem)
            combine()

        @pl.when(i + AHEAD < na)
        def _():
            send_x(i + AHEAD)

        @pl.when((i > 0) & (i % B_EVERY == 0) & (i // B_EVERY < N_B))
        def _():
            send_b(i // B_EVERY)

        @pl.when(i < na)
        def _():
            x_copy(i).wait_recv()

            def one(d, c):
                for j in range(tpc):
                    xrecv[i, d, j] = (part(i, 2 * d + x, j) + xrecv[i, d, j].astype(F32)).astype(BF16)
                return c

            lax.fori_loop(0, n, one, 0)

            @pl.when(z == 0)
            def _():
                for d in range(last, 0, -1):
                    up_copy(xrecv, i, d).start()

            @pl.when(z == last)
            def _():
                for d in range(last):
                    down_copy(xrecv, i, d).start()

        q = i - LAG * z

        @pl.when((z > 0) & (z < last) & (q >= 0) & (q < na))
        def _():
            for d in range(last, 1, -1):
                @pl.when(d > z)
                def _():
                    up_copy(up, q, d).wait_recv()
                    add_into(up.at[q, d], xrecv.at[q, d])
                    up_copy(up, q, d).start()

        w = i - LAG * (last - z)

        @pl.when((z > 0) & (z < last) & (w >= 0) & (w < na))
        def _():
            for d in range(last - 1):
                @pl.when(d < z)
                def _():
                    down_copy(down, w, d).wait_recv()
                    add_into(down.at[w, d], xrecv.at[w, d])
                    down_copy(down, w, d).start()

        f = i - LAG * last

        @pl.when((f >= 0) & (f < na))
        def _():
            @pl.when(z > 0)
            def _():
                up_copy(up, f, z).wait_recv()

            @pl.when(z < last)
            def _():
                down_copy(down, f, z).wait_recv()

            for j in range(tpc):
                total = xrecv[f, z, j].astype(F32)
                total += jnp.where(z > 0, up[f, z, j].astype(F32), 0.0)
                total += jnp.where(z < last, down[f, z, j].astype(F32), 0.0)
                out_ref[f, :, j * tw:(j + 1) * tw] = (total / n_rep).astype(BF16)

        bu = i - B_LAG * z

        @pl.when((z > 0) & (z < last) & (bu >= 0) & (bu % B_EVERY == 0) & (bu // B_EVERY < N_B))
        def _():
            k = bu // B_EVERY
            for d in range(last, 1, -1):
                @pl.when(d > z)
                def _():
                    upb_copy(up_b, k, d).wait_recv()
                    for c in range(2):
                        add_into(up_b.at[k, d, c], own_b.at[k, d, c])
                    upb_copy(up_b, k, d).start()

        bd = i - B_LAG * (last - z)

        @pl.when((z > 0) & (z < last) & (bd >= 0) & (bd % B_EVERY == 0) & (bd // B_EVERY < N_B))
        def _():
            k = bd // B_EVERY
            for d in range(last - 1):
                @pl.when(d < z)
                def _():
                    downb_copy(down_b, k, d).wait_recv()
                    for c in range(2):
                        add_into(down_b.at[k, d, c], own_b.at[k, d, c])
                    downb_copy(down_b, k, d).start()

        bf = i - B_LAG * last

        @pl.when((bf >= 0) & (bf % B_EVERY == 0) & (bf // B_EVERY < N_B))
        def _():
            k = bf // B_EVERY

            @pl.when(z > 0)
            def _():
                upb_copy(up_b, k, z).wait_recv()

            @pl.when(z < last)
            def _():
                downb_copy(down_b, k, z).wait_recv()

            def total(c, j):
                t = own_b[k, z, c, j].astype(F32)
                t += jnp.where(z > 0, up_b[k, z, c, j].astype(F32), 0.0)
                return t + jnp.where(z < last, down_b[k, z, c, j].astype(F32), 0.0)

            for j in range(tpc):
                xs_b[k, j] = total(1 - x, j).astype(BF16)
            xb_copy(k).start()
            for j in range(tpc):
                own_b[k, z, x, j] = total(x, j).astype(BF16)

        return carry

    steps = max(na + LAG * last, B_EVERY * (N_B - 1) + B_LAG * last + 1)
    lax.fori_loop(0, steps, step, 0)

    def finish_b(k, carry):
        xb_copy(k).wait_recv()
        for j in range(tpc):
            total = own_b[k, z, x, j].astype(F32) + xr_b[k, j].astype(F32)
            out_ref[na + k, :, j * tw:(j + 1) * tw] = (total / n_rep).astype(BF16)
        xb_copy(k).wait_send()
        return carry

    lax.fori_loop(0, N_B, finish_b, 0)

    def drain(i, carry):
        x_copy(i).wait_send()

        @pl.when(z < last)
        def _():
            for d in range(1, n):
                @pl.when(d > z)
                def _():
                    up_copy(up, i, d).wait_send()

        @pl.when(z > 0)
        def _():
            for d in range(last):
                @pl.when(d < z)
                def _():
                    down_copy(down, i, d).wait_send()

        return carry

    lax.fori_loop(0, na, drain, 0)

    def drain_b(k, carry):
        @pl.when(z < last)
        def _():
            for d in range(1, n):
                @pl.when(d > z)
                def _():
                    upb_copy(up_b, k, d).wait_send()

        @pl.when(z > 0)
        def _():
            for d in range(last):
                @pl.when(d < z)
                def _():
                    downb_copy(down_b, k, d).wait_send()

        return carry

    lax.fori_loop(0, N_B, drain_b, 0)


def reduce_deltas(left, right, parts, home, gate, n_rep, columns):
    n = n_rep // 2
    pr, depth = left.shape[2:]
    tw = right.shape[2]
    tpc = columns // tw
    na = PIECES - N_B
    chunk = (tpc, pr, tw)
    dma = pltpu.SemaphoreType.DMA
    vmem = pl.BlockSpec(memory_space=pltpu.VMEM)
    n_exp = parts.shape[0]
    out, mixed = pl.pallas_call(
        functools.partial(reduce_kernel, n, n_exp),
        out_shape=(
            jax.ShapeDtypeStruct((PIECES, pr, columns), BF16),
            jax.ShapeDtypeStruct((gate.shape[0], parts.shape[2]), BF16),
        ),
        in_specs=[vmem] * 5,
        out_specs=(vmem, vmem),
        scratch_shapes=[
            pltpu.VMEM(parts.shape, BF16),
            dma((n_exp - 1,)),
            dma((n_exp - 1,)),
            pltpu.VMEM((na, n) + chunk, BF16),
            pltpu.VMEM((na, n) + chunk, BF16),
            pltpu.VMEM((na, n) + chunk, BF16),
            pltpu.VMEM((na, n) + chunk, BF16),
            pltpu.VMEM((N_B, n, 2) + chunk, BF16),
            pltpu.VMEM((N_B, n, 2) + chunk, BF16),
            pltpu.VMEM((N_B, n, 2) + chunk, BF16),
            pltpu.VMEM((N_B,) + chunk, BF16),
            pltpu.VMEM((N_B,) + chunk, BF16),
            dma((na,)),
            dma((na,)),
            dma((na, n)),
            dma((na, n)),
            dma((na, n)),
            dma((na, n)),
            dma((N_B, n)),
            dma((N_B, n)),
            dma((N_B, n)),
            dma((N_B, n)),
            dma((N_B,)),
            dma((N_B,)),
        ],
        compiler_params=pltpu.CompilerParams(
            collective_id=0, has_side_effects=True, vmem_limit_bytes=56 * 2**20
        ),
        cost_estimate=pl.CostEstimate(
            flops=2 * 3 * PIECES * pr * depth * columns * n_rep // 3,
            bytes_accessed=8 * 2**20, transcendentals=0,
        ),
    )(left, right, parts, home, gate)
    return out.reshape(PIECES * pr, columns), mixed


def body(tokens, expert_ids, gate_prob, cotangent, w_gate, w_up, w_down, touched):
    rows = tokens.shape[0]
    width = tokens.shape[1]
    n_exp = lax.axis_size("exp")
    n_rep = lax.axis_size("rep")
    cap = rows // EW
    onehot = (expert_ids == jnp.arange(EW)[None, :]).astype(jnp.float32)
    lower = (
        lax.broadcasted_iota(jnp.int32, (rows, rows), 0)
        > lax.broadcasted_iota(jnp.int32, (rows, rows), 1)
    ).astype(jnp.float32)
    earlier = jnp.dot(lower, onehot, precision=lax.Precision.HIGHEST)
    slot_of = jnp.sum(onehot * earlier, axis=1).astype(jnp.int32)
    target = expert_ids[:, 0] * cap + slot_of
    placer = (target[None, :] == jnp.arange(EW * cap)[:, None]).astype(jnp.bfloat16)
    columns = 3 * width // n_rep
    tw = math.gcd(columns, width)
    recv, right = dispatch(tokens, cotangent, gate_prob[:, None], placer, n_exp, tw)
    recv = recv.reshape(n_exp * cap, 2 * width)
    right = right.reshape(2 * width // tw, n_exp * cap, tw)
    x_rows = recv[:, :width]
    d_rows = recv[:, width:]
    wg = w_gate[0]
    wu = w_up[0]
    wd = w_down[0]
    h = jnp.dot(x_rows, wg, preferred_element_type=jnp.float32)
    u = jnp.dot(x_rows, wu, preferred_element_type=jnp.float32)
    act = (h * jax.nn.sigmoid(h) * u).astype(jnp.bfloat16)
    partial_out = jnp.dot(act, wd, preferred_element_type=jnp.float32).astype(jnp.bfloat16)
    grad_a = lax.dot_general(
        d_rows, wd, (((1,), (1,)), ((), ())), preferred_element_type=jnp.float32
    )
    d_h = (grad_a * u * swish_slope(h)).astype(jnp.bfloat16)
    d_u = (grad_a * h * jax.nn.sigmoid(h)).astype(jnp.bfloat16)
    hidden = d_h.shape[1]
    mask = jnp.repeat(touched[0], TILE).astype(jnp.bfloat16)
    left = (jnp.stack([d_h, d_u, act]) * mask[None, None, :]).transpose(0, 2, 1)
    left = left.reshape(3, PIECES, hidden // PIECES, left.shape[2])
    home = (
        target[None, :, None] == jnp.arange(EW * cap).reshape(EW, 1, cap)
    ).astype(jnp.bfloat16)
    averaged, mixed = reduce_deltas(
        left, right, partial_out.reshape(n_exp, cap, width), home, gate_prob[:, None],
        n_rep, columns,
    )
    return (mixed, averaged)


def solution(mesh):
    return jax.shard_map(
        body,
        mesh=mesh,
        in_specs=(
            P(("rep", "exp"), None),
            P(("rep", "exp"), None),
            P(("rep", "exp")),
            P(("rep", "exp"), None),
            P("rep", None, "exp"),
            P("rep", None, "exp"),
            P("rep", "exp", None),
            P("rep", "exp"),
        ),
        out_specs=(P(("rep", "exp"), None), P("exp", "rep")),
        check_vma=False,
    )
```
